512 devices in a mesh: req: 64 (over z, x, core), tensor: 8 (over y).
Axes of the slice: x: 4, y: 8, z: 8, core: 2. Of those that a mesh axis runs over, the one named last changes fastest.
Arguments:
- prompts: bfloat16 [32768, 4096], P(('req', 'tensor')), may hold values from -6 to 6
- layer_norm_gain: float32 [4096], replicated, may hold values from 0.1 to 1.9
- query_base_matrix: bfloat16 [4096, 4096], P('req', 'tensor'), may hold values from -0.09375 to 0.09375
- adapter_down_weight: bfloat16 [128, 32, 4096], P('req', None, 'tensor'), may hold values from -0.09375 to 0.09375
- adapter_up_weight: bfloat16 [128, 32, 4096], P('req', None, 'tensor'), may hold values from -1 to 1
- request_prompt_length: int32 [64], P('req'), may hold values from 128 to 512, as said below
- request_adapter_ident: int32 [64], P('req'), may hold values from 0 to 127
- adapter_pool_row: int32 [128], replicated, may hold values from 0 to 127, each once
Outputs:
- queries: bfloat16 [32768, 4096], P('req', 'tensor')
The draws below stay inside these ranges and needn't reach their ends.
Inputs may be any that keep to these rules, and one draw needn't show every extreme that they name: `request_prompt_length`: lengths lie between 128 and 512; some request has exactly 512.
All inputs are finite; a program needn't handle non-finite values.
Results may differ from the reference program's by a relative error of at most 0.0054.
Values may be sent and summed in bfloat16 or wider, within the bound.
No kernel may reach another device: no remote copies, remote signals or barrier semaphores. Data moves between devices by JAX's collectives and lax.ppermute only.
A program may use at most 64 MiB of HBM per device.

```python
import math
import jax
import jax.numpy as jnp
import numpy as np
from jax import lax

MODEL_WIDTH = 4096
ADAPTER_RANK = 32
LMAX = 512
REQUESTS = 64
ADAPTER_COUNT = 128
TOKENS = 32768


def draw_request_prompt_length(key, part):
    key = jax.random.fold_in(key, 3)
    values = jax.random.randint(key, (REQUESTS,), LMAX // 4, LMAX + 1, dtype=jnp.int32)
    return values.at[0].set(LMAX)


def with_ends(drawn, stream_key, least, top_value):
    index_at = [jax.random.randint(jax.random.fold_in(stream_key, axis), (), 0, length) for axis, length in enumerate(drawn.shape)]
    main_axis = drawn.shape.index(max(drawn.shape))
    next_to = index_at[:main_axis] + [(index_at[main_axis] + 1) % drawn.shape[main_axis]] + index_at[main_axis + 1:]
    return drawn.at[tuple(index_at)].set(least).at[tuple(next_to)].set(top_value)


def shard_levels(rng, dims, shards, least, top_value):
    def one(position, shards_of):
        steps = jax.random.uniform(jax.random.fold_in(jax.random.fold_in(rng, 6), position), (shards_of,), jnp.float32, least / len(shards), top_value / len(shards))
        return jnp.repeat(jnp.exp(steps), dims[position] // shards_of).reshape((-1,) + (1,) * (len(dims) - position - 1))

    gain = one(*shards[0])
    for cut in shards[1:]:
        gain = gain * one(*cut)
    return gain


def cumulative_ranks(number_of, skew):
    portions = [(1 << 20) // math.isqrt(rank ** skew) + 1 for rank in range(1, number_of + 1)]
    spread = 1 + sum(portions) // (1 << 30)
    return np.cumsum(np.array([max(1, weight // spread) for weight in portions]))


def ranked_ids(stream_key, extent, count, skew):
    listing = cumulative_ranks(count, skew)
    pick = jax.random.randint(jax.random.fold_in(stream_key, 1), extent, 0, int(listing[count - 1]))
    rank = jnp.searchsorted(jnp.asarray(listing, jnp.int32), pick, side="right")
    return jax.random.permutation(jax.random.fold_in(stream_key, 2), count)[rank].astype(jnp.int32)


def gaussian(stream_key, extent, spread, most, cuts=(), held_as=jnp.bfloat16):
    drawn = jax.random.normal(stream_key, extent, jnp.float32) * spread
    if len(cuts) > 0:
        drawn = shard_levels(stream_key, extent, cuts, -0.22, 0.18) * drawn
    return jnp.clip(drawn, min=-most, max=most).astype(held_as)


def setup_inputs(seed: int = 0) -> dict:
    streams_of = jax.random.split(jax.random.key(seed), 9)
    prompts = gaussian(streams_of[0], (TOKENS, MODEL_WIDTH), 1.0, 6.0, ((0, 512),))
    layer_norm_gain = jnp.clip(1.0 + 0.18 * jax.random.normal(streams_of[1], (MODEL_WIDTH,), jnp.float32), 0.1, 1.9)
    query_base_matrix = gaussian(streams_of[2], (MODEL_WIDTH, MODEL_WIDTH), MODEL_WIDTH ** -0.5, 0.09375, ((0, 64), (1, 8)))
    adapter_down_weight = gaussian(streams_of[3], (ADAPTER_COUNT, ADAPTER_RANK, MODEL_WIDTH), MODEL_WIDTH ** -0.5, 0.09375, ((0, 64), (2, 8)))
    adapter_up_weight = gaussian(streams_of[4], (ADAPTER_COUNT, ADAPTER_RANK, MODEL_WIDTH), ADAPTER_RANK ** -0.5, 1.0, ((0, 64), (2, 8)))
    request_prompt_length = draw_request_prompt_length(jax.random.fold_in(streams_of[8], 71), 0)
    request_adapter_ident = with_ends(ranked_ids(streams_of[6], (REQUESTS,), ADAPTER_COUNT, 2), jax.random.fold_in(streams_of[6], 3), 0, ADAPTER_COUNT - 1).astype(jnp.int32)
    adapter_pool_row = jax.random.permutation(streams_of[7], ADAPTER_COUNT).astype(jnp.int32)
    return {"prompts": prompts, "layer_norm_gain": layer_norm_gain, "query_base_matrix": query_base_matrix, "adapter_down_weight": adapter_down_weight, "adapter_up_weight": adapter_up_weight, "request_prompt_length": request_prompt_length, "request_adapter_ident": request_adapter_ident, "adapter_pool_row": adapter_pool_row}


def normalize(rows, layer_norm_gain):
    values = rows.astype(jnp.float32)
    scale = lax.rsqrt(lax.optimization_barrier(jnp.mean(values * values, axis=-1, keepdims=True)) + 1e-06)
    return (values * scale * layer_norm_gain).astype(jnp.bfloat16)

def reference(prompts, layer_norm_gain, query_base_matrix, adapter_down_weight, adapter_up_weight, request_prompt_length, request_adapter_ident, adapter_pool_row):
    slots = adapter_pool_row[request_adapter_ident].astype(jnp.int32)
    blocks = prompts.reshape(REQUESTS, LMAX, MODEL_WIDTH)

    def single(items):
        rows, pool_row_index, length = items
        normed = normalize(rows, layer_norm_gain)
        base = jnp.dot(normed, query_base_matrix, preferred_element_type=jnp.float32)
        down_matrix = lax.dynamic_index_in_dim(adapter_down_weight, pool_row_index, 0, keepdims=False)
        up_matrix = lax.dynamic_index_in_dim(adapter_up_weight, pool_row_index, 0, keepdims=False)
        low = jnp.dot(normed, down_matrix.T, preferred_element_type=jnp.float32).astype(jnp.bfloat16)
        total = base + jnp.dot(low, up_matrix, preferred_element_type=jnp.float32)
        valid = jnp.arange(LMAX, dtype=jnp.int32) < length
        return jnp.where(valid[:, None], total, 0.0).astype(jnp.bfloat16)
    return lax.map(single, (blocks, slots, request_prompt_length)).reshape(TOKENS, MODEL_WIDTH)
```

```python
import functools

import jax
import jax.numpy as jnp
from jax import lax
from jax.experimental import pallas as pl
from jax.experimental.pallas import tpu as pltpu
from jax.sharding import PartitionSpec as P

Z, X, C, Y = 8, 4, 2, 8
RING = (-3, 0, 3, -4, -1, 2, -2, 1)
QUAD = (0, -1, 1, 2)


def req_pairs(dz=0, dx=0, dc=0):
    return [
        ((z * X + x) * C + c, (((z + dz) % Z) * X + (x + dx) % X) * C + (c + dc) % C)
        for z in range(Z)
        for x in range(X)
        for c in range(C)
    ]


def shift(value, **by):
    return lax.ppermute(value, "req", req_pairs(**by))


def shift_y(value, by):
    return lax.ppermute(value, "tensor", [(y, (y + by) % Y) for y in range(Y)])


def ring_gather(value, move):
    trio = jnp.concatenate([move(value, 3), value, move(value, -3)], axis=0)
    n = value.shape[0]
    before = move(trio, 1)
    after = move(trio[: 2 * n], -1)
    return jnp.concatenate([trio, before, after], axis=0)


def normalize(rows, layer_norm_gain):
    values = rows.astype(jnp.float32)
    scale = lax.rsqrt(jnp.mean(values * values, axis=-1, keepdims=True) + 1e-06)
    return (values * scale * layer_norm_gain).astype(jnp.bfloat16)


def pick_kernel(place_ref, mine_ref, other_ref, minus_ref, plus_ref, own_ref, sems):
    outs = [(minus_ref, i) for i in range(3)] + [(plus_ref, i) for i in range(2)] + [(own_ref, i) for i in range(3)]
    for n, (ref, i) in enumerate(outs):
        side, at = place_ref[2 * n], place_ref[2 * n + 1]

        @pl.when(side == 0)
        def _(ref=ref, i=i, at=at, n=n):
            pltpu.make_async_copy(mine_ref.at[at], ref.at[i], sems.at[n]).start()

        @pl.when(side != 0)
        def _(ref=ref, i=i, at=at, n=n):
            pltpu.make_async_copy(other_ref.at[at], ref.at[i], sems.at[n]).start()

    for n, (ref, i) in enumerate(outs):
        pltpu.make_async_copy(mine_ref.at[0], ref.at[i], sems.at[n]).wait()


def project_kernel(at_ref, rows_ref, mine_ref, other_ref, down_ref, up_ref, out_ref, rows, weight, down, acc, row_sems, weight_sems, down_sems):
    z, x, c, y, length = (at_ref[i] for i in range(5))
    copies = []
    for j, dz in enumerate(RING):
        feature = lax.rem(z + dz + Z, Z)
        here = []
        for s, side in enumerate((mine_ref, other_ref)):
            for q, dx in enumerate(QUAD):
                to = lax.rem(x + dx + X, X) * C + lax.rem(c + s, C)
                here.append(
                    pltpu.make_async_copy(
                        side.at[pl.ds((q * Z + j) * 64, 64)],
                        weight.at[j, pl.ds(pl.multiple_of(to * 64, 64), 64)],
                        weight_sems.at[j * 8 + s * 4 + q],
                    )
                )
        here.append(
            pltpu.make_async_copy(
                rows_ref.at[:, pl.ds(pl.multiple_of(feature * 512, 512), 512)], rows.at[j], row_sems.at[j]
            )
        )
        for copy in here:
            copy.start()
        copies.append(here)
    down_copies = []
    for j, dy in enumerate(RING):
        to = lax.rem(y + dy + Y, Y)
        down_copies.append(pltpu.make_async_copy(down_ref.at[pl.ds(j * 32, 32)], down.at[to], down_sems.at[j]))
        down_copies[-1].start()
    for copy in down_copies:
        copy.wait()
    low = jnp.zeros((rows.shape[1], 32), jnp.float32)
    for j, dz in enumerate(RING):
        feature = lax.rem(z + dz + Z, Z)
        for copy in copies[j]:
            copy.wait()
        term = jnp.dot(rows[j], weight[j], preferred_element_type=jnp.float32)
        if j == 0:
            acc[...] = term
        else:
            acc[...] += term
        low += lax.dot_general(rows[j], down[feature], (((1,), (1,)), ((), ())), preferred_element_type=jnp.float32)
    total = acc[...] + jnp.dot(low.astype(jnp.bfloat16), up_ref[...], preferred_element_type=jnp.float32)
    valid = lax.broadcasted_iota(jnp.int32, total.shape, 0) < length
    out_ref[...] = jnp.where(valid, total, 0.0).astype(jnp.bfloat16)


def per_device(
    prompts,
    layer_norm_gain,
    query_base_matrix,
    adapter_down_weight,
    adapter_up_weight,
    request_prompt_length,
    request_adapter_ident,
    adapter_pool_row,
):
    req, y = lax.axis_index("req"), lax.axis_index("tensor")
    z, x, c = req // (X * C), (req // C) % X, req % C
    normed = lax.all_gather(normalize(prompts, layer_norm_gain), "tensor", axis=0, tiled=True)

    hits = request_adapter_ident[:, None] == jnp.arange(adapter_pool_row.shape[0], dtype=jnp.int32)[None, :]
    slot = jnp.sum(jnp.where(hits, adapter_pool_row[None, :], 0))

    noted = jnp.full((16, 512), slot, jnp.bfloat16)
    ring = ring_gather(jnp.concatenate([query_base_matrix, noted], axis=0), lambda v, k: shift(v, dz=k))
    ring = ring.reshape(Z, 80, 512)
    ring_slots = ring[:, 64, 0].astype(jnp.int32)
    wanted = {dz % Z: ring_slots[j] for j, dz in enumerate(RING)}
    weight = ring[:, :64].reshape(512, 512)
    from_left, from_right = shift(weight, dx=1), shift(weight, dx=-1)
    far_pairs = [p for p in req_pairs(dx=1) if p[0] % C == 0] + [p for p in req_pairs(dx=-1) if p[0] % C == 1]
    far = lax.ppermute(jnp.where(c == 0, from_left, from_right), "req", far_pairs)
    mine = jnp.concatenate([weight, from_left, from_right, far], axis=0)
    other = shift(mine, dc=1)

    own = jnp.concatenate([adapter_down_weight, adapter_up_weight], axis=1)
    plane = jnp.concatenate([own, shift(own, dx=1), shift(own, dx=-1), shift(own, dx=2)], axis=0)
    plane_other = shift(plane, dc=1)
    place = []
    for d in (-1, -4, 2, 1, -2, 0, 3, -3):
        s = wanted[d % Z]
        owner = (s // 2) % (X * C)
        dx = (owner // C - x) % X
        at = jnp.where(dx == 0, 0, jnp.where(dx == 3, 1, jnp.where(dx == 1, 2, 3))) * 2 + s % 2
        place += [(owner % C != c).astype(jnp.int32), at]
    slab = jax.ShapeDtypeStruct((3, 64, 512), jnp.bfloat16)
    minus, plus, kept = pl.pallas_call(
        pick_kernel,
        out_shape=(slab, jax.ShapeDtypeStruct((2, 64, 512), jnp.bfloat16), slab),
        in_specs=[pl.BlockSpec(memory_space=pltpu.SMEM)] + [pl.BlockSpec(memory_space=pl.ANY)] * 2,
        out_specs=[pl.BlockSpec(memory_space=pl.ANY)] * 3,
        scratch_shapes=[pltpu.SemaphoreType.DMA((8,))],
        name="pick_adapters",
    )(jnp.stack(place), plane, plane_other)
    above = shift(minus, dz=-1)
    below = shift(plus, dz=1)

    def nearest(d, own_part, below_part, above_part):
        rel = (wanted[d % Z] // (2 * X * C) - z) % Z
        return jnp.where(rel == 0, own_part, jnp.where(rel == 1, above_part, below_part))

    near = nearest(0, kept[0], below[0], above[0])
    to_plus = nearest(3, kept[1], above[2], above[2])
    to_minus = nearest(-3, kept[2], below[1], above[1])
    from_minus = shift(to_plus, dz=3)
    from_plus = shift(to_minus, dz=-3)
    gone = (z - wanted[0] // (2 * X * C)) % Z
    adapter = jnp.where((gone <= 1) | (gone == 7), near, jnp.where((gone == 2) | (gone == 3), from_minus, from_plus))
    down = ring_gather(adapter[:32], shift_y)

    at = jnp.stack([z, x, c, y, request_prompt_length[0]]).astype(jnp.int32)
    return pl.pallas_call(
        project_kernel,
        out_shape=jax.ShapeDtypeStruct((512, 512), jnp.bfloat16),
        in_specs=[pl.BlockSpec(memory_space=pltpu.SMEM)]
        + [pl.BlockSpec(memory_space=pl.ANY)] * 4
        + [pl.BlockSpec(memory_space=pltpu.VMEM)],
        out_specs=pl.BlockSpec(memory_space=pltpu.VMEM),
        scratch_shapes=[
            pltpu.VMEM((8, 512, 512), jnp.bfloat16),
            pltpu.VMEM((8, 512, 512), jnp.bfloat16),
            pltpu.VMEM((8, 32, 512), jnp.bfloat16),
            pltpu.VMEM((512, 512), jnp.float32),
            pltpu.SemaphoreType.DMA((8,)),
            pltpu.SemaphoreType.DMA((64,)),
            pltpu.SemaphoreType.DMA((8,)),
        ],
        compiler_params=pltpu.CompilerParams(vmem_limit_bytes=32 * 1024 * 1024),
        cost_estimate=pl.CostEstimate(flops=2 * 512 * 4096 * 544, bytes_accessed=9 << 20, transcendentals=0),
        name="project",
    )(at, normed, mine, other, down, adapter[32:])


def solution(mesh):
    in_specs = (
        P(("req", "tensor"), None),
        P(),
        P("req", "tensor"),
        P("req", None, "tensor"),
        P("req", None, "tensor"),
        P("req"),
        P("req"),
        P(),
    )
    out_specs = P("req", "tensor")
    return jax.shard_map(
        per_device, mesh=mesh, in_specs=in_specs, out_specs=out_specs, check_vma=False
    )
```

```python
import jax
import jax.numpy as jnp
from jax import lax
from jax.experimental import pallas as pl
from jax.experimental.pallas import tpu as pltpu
from jax.sharding import PartitionSpec as P

RING = (-3, 0, 3, -4, -1, 2, -2, 1)
QUAD = (0, -1, 1, 2)
Z, X, C, Y = 8, 4, 2, 8
REQ = ("z", "x", "c")


def after(value, *others):
    return lax.optimization_barrier((value, *others))[0]


def to_all(value, axis, size):
    return lax.all_to_all(jnp.broadcast_to(value, (size, *value.shape)), axis, 0, 0)


def req_pairs(dz=0, dx=0):
    return [
        ((z * X + x) * C + c, (((z + dz) % Z) * X + (x + dx) % X) * C + c)
        for z in range(Z)
        for x in range(X)
        for c in range(C)
    ]


def shift(value, **by):
    return lax.ppermute(value, REQ, req_pairs(**by))


def shift_y(value, by):
    return lax.ppermute(value, "y", [(y, (y + by) % Y) for y in range(Y)])


def swap(value):
    return lax.ppermute(value, "c", [(0, 1), (1, 0)])


def prepare_kernel(ident_ref, pool_ref, rows_ref, gain_ref, base_ref, down_ref, up_ref, rows_out, base_out, pair_out):
    base_out[:64] = base_ref[...]
    base_out[64:] = jnp.full((16, 512), pool_ref[ident_ref[0]].astype(jnp.float32)).astype(jnp.bfloat16)
    values = rows_ref[...].astype(jnp.float32)
    scale = lax.rsqrt(jnp.mean(values * values, axis=-1, keepdims=True) + 1e-06)
    rows_out[...] = (values * scale * gain_ref[...]).astype(jnp.bfloat16)
    pair_out[:, :32] = down_ref[...]
    pair_out[:, 32:] = up_ref[...]


def pick_kernel(slots_ref, mine_ref, other_ref, out_ref):
    z, c = lax.axis_index("z"), lax.axis_index("c")
    for j, dz in enumerate(RING):
        slot = slots_ref[j]
        owner = lax.rem(lax.div(slot, 2), X * C)
        at = lax.div(owner, C) * 2 + lax.rem(slot, 2)
        to = lax.rem(z + dz + Z, Z)

        @pl.when(lax.rem(owner, C) == c)
        def _(to=to, at=at):
            out_ref[to] = mine_ref[at]

        @pl.when(lax.rem(owner, C) != c)
        def _(to=to, at=at):
            out_ref[to] = other_ref[at]


def bf16(*shape):
    return jax.ShapeDtypeStruct(shape, jnp.bfloat16)


def small(kernel, name, out_shape, scalars, *arrays):
    smem, vmem = pl.BlockSpec(memory_space=pltpu.SMEM), pl.BlockSpec(memory_space=pltpu.VMEM)
    return pl.pallas_call(
        kernel,
        out_shape=out_shape,
        in_specs=[smem] * len(scalars) + [vmem] * len(arrays),
        out_specs=[vmem] * len(out_shape),
        cost_estimate=pl.CostEstimate(flops=0, bytes_accessed=2 << 20, transcendentals=0),
        name=name,
    )(*scalars, *arrays)


def project_kernel(length_ref, *refs):
    row_refs, (mine_ref, other_ref, down, up_ref, out_ref, rows, weight, acc, row_sems, weight_sems) = refs[:-10], refs[-10:]
    c = lax.axis_index("c")
    row_copies = [pltpu.make_async_copy(row_refs[0], rows, row_sems.at[0])]
    for copy in row_copies:
        copy.start()
    z, x = lax.axis_index("z"), lax.axis_index("x")
    copies = [[] for _ in range(Z)]
    for j, dz in enumerate(RING):
        to_z = lax.rem(z + dz + Z, Z)
        for s, side in enumerate((mine_ref, other_ref)):
            for q, dx in enumerate(QUAD):
                to = (lax.rem(x + dx + X, X) * C + lax.rem(c + s, C)) * 64
                copies[j].append(
                    pltpu.make_async_copy(
                        side.at[pl.ds((q * Z + j) * 64, 64)],
                        weight.at[j, pl.ds(pl.multiple_of(to, 64), 64)],
                        weight_sems.at[j * 8 + s * 4 + q],
                    )
                )
                copies[j][-1].start()
    for copy in row_copies:
        copy.wait()
    low = jnp.zeros((512, 32), jnp.float32)
    for j, dz in enumerate(RING):
        to_z = lax.rem(z + dz + Z, Z)
        for copy in copies[j]:
            copy.wait()
        part = rows[:, pl.ds(pl.multiple_of(to_z * 512, 512), 512)]
        term = jnp.dot(part, weight[j], preferred_element_type=jnp.float32)
        if j == 0:
            acc[...] = term
        else:
            acc[...] += term
        low += lax.dot_general(part, down[to_z], (((1,), (1,)), ((), ())), preferred_element_type=jnp.float32)
    total = acc[...] + jnp.dot(low.astype(jnp.bfloat16), up_ref[...], preferred_element_type=jnp.float32)
    valid = lax.broadcasted_iota(jnp.int32, total.shape, 0) < length_ref[0]
    out_ref[...] = jnp.where(valid, total, 0.0).astype(jnp.bfloat16)


def per_device(
    prompts,
    layer_norm_gain,
    query_base_matrix,
    adapter_down_weight,
    adapter_up_weight,
    request_prompt_length,
    request_adapter_ident,
    adapter_pool_row,
):
    rows, noted, own = small(
        prepare_kernel,
        "prepare",
        (bf16(64, 4096), bf16(80, 512), bf16(2, 64, 512)),
        (request_adapter_ident, adapter_pool_row),
        prompts,
        layer_norm_gain.reshape(1, -1),
        query_base_matrix,
        adapter_down_weight,
        adapter_up_weight,
    )
    normed = (lax.all_gather(rows, "y", axis=0, tiled=True),)
    plane = to_all(own, "x", X).reshape(X * 2, 64, 512)
    trio = jnp.concatenate([shift(noted, dz=3), noted, shift(noted, dz=-3)], axis=0)
    plane, trio = lax.optimization_barrier((plane, trio))

    plane_other = swap(plane)
    ring = jnp.concatenate([trio, shift(trio, dz=1), shift(trio[:160], dz=-1)], axis=0)
    plane_other, ring = lax.optimization_barrier((plane_other, ring))
    ring = ring.reshape(Z, 80, 512)
    slots, weight = ring[:, 64, 0].astype(jnp.int32), ring[:, :64].reshape(512, 512)

    (wanted,) = small(pick_kernel, "pick", (bf16(Z, 64, 512),), (slots,), plane, plane_other)
    wanted, weight = lax.optimization_barrier((wanted, weight))
    planes = lax.all_to_all(wanted, "z", 0, 0)
    from_left, from_right = shift(weight, dx=1), shift(weight, dx=-1)
    core = lax.axis_index("c")
    far_pairs = [p for p in req_pairs(dx=1) if p[0] % C == 0] + [p for p in req_pairs(dx=-1) if p[0] % C == 1]
    planes, from_left, from_right = lax.optimization_barrier((planes, from_left, from_right))
    far = lax.ppermute(jnp.where(core == 0, from_left, from_right), REQ, far_pairs)

    adapter = lax.dynamic_index_in_dim(planes, slots[RING.index(0)] // (2 * X * C), 0, keepdims=False)
    spread = jnp.broadcast_to(adapter[:32], (Y, 32, 512))
    far, spread = lax.optimization_barrier((far, spread))
    down, up = lax.all_to_all(spread, "y", 0, 0), adapter[32:]
    mine = jnp.concatenate([weight, from_left, from_right, far], axis=0)
    other = swap(mine)

    any_space, vmem = pl.BlockSpec(memory_space=pl.ANY), pl.BlockSpec(memory_space=pltpu.VMEM)
    return pl.pallas_call(
        project_kernel,
        out_shape=bf16(512, 512),
        in_specs=[pl.BlockSpec(memory_space=pltpu.SMEM)] + [any_space] * (len(normed) + 2) + [vmem] * 2,
        out_specs=vmem,
        scratch_shapes=[
            pltpu.VMEM((512, 4096), jnp.bfloat16),
            pltpu.VMEM((8, 512, 512), jnp.bfloat16),
            pltpu.VMEM((512, 512), jnp.float32),
            pltpu.SemaphoreType.DMA((9,)),
            pltpu.SemaphoreType.DMA((64,)),
        ],
        compiler_params=pltpu.CompilerParams(vmem_limit_bytes=60 * 1024 * 1024),
        cost_estimate=pl.CostEstimate(flops=2 * 512 * 4096 * 544, bytes_accessed=9 << 20, transcendentals=0),
        name="project",
    )(request_prompt_length, *normed, mine, other, down, up)


def solution(mesh):
    mesh = jax.sharding.Mesh(mesh.devices.reshape(Z, X, C, Y), (*REQ, "y"))
    in_specs = (
        P((*REQ, "y"), None),
        P(),
        P(REQ, "y"),
        P(REQ, None, "y"),
        P(REQ, None, "y"),
        P(REQ),
        P(REQ),
        P(),
    )
    return jax.shard_map(
        per_device, mesh=mesh, in_specs=in_specs, out_specs=P(REQ, "y"), check_vma=False
    )
```

```python
import jax
import jax.numpy as jnp
from jax import lax
from jax.experimental import pallas as pl
from jax.experimental.pallas import tpu as pltpu
from jax.sharding import PartitionSpec as P

QUAD = (0, -1, 1, 2)
Z, X, C, Y = 8, 4, 2, 8
REQ = ("z", "x", "c")


def after(value, *others):
    return lax.optimization_barrier((value, *others))[0]


def to_all(value, axis, size):
    return lax.all_to_all(jnp.broadcast_to(value, (size, *value.shape)), axis, 0, 0)


def req_pairs(dz=0, dx=0):
    return [
        ((z * X + x) * C + c, (((z + dz) % Z) * X + (x + dx) % X) * C + c)
        for z in range(Z)
        for x in range(X)
        for c in range(C)
    ]


def shift(value, **by):
    return lax.ppermute(value, REQ, req_pairs(**by))


def shift_y(value, by):
    return lax.ppermute(value, "y", [(y, (y + by) % Y) for y in range(Y)])


def swap(value):
    return lax.ppermute(value, "c", [(0, 1), (1, 0)])


def prepare_kernel(ident_ref, pool_ref, rows_ref, gain_ref, weight_ref, down_ref, up_ref, rows_out, weight_out, pair_out):
    slot = jnp.full((16, 512), pool_ref[ident_ref[0]].astype(jnp.float32)).astype(jnp.bfloat16)
    for z in range(Z):
        weight_out[z, :64] = weight_ref[...]
        weight_out[z, 64:] = slot
    values = rows_ref[...].astype(jnp.float32)
    scale = lax.rsqrt(jnp.mean(values * values, axis=-1, keepdims=True) + 1e-06)
    rows_out[...] = (values * scale * gain_ref[...]).astype(jnp.bfloat16)
    pair_out[:, :32] = down_ref[...]
    pair_out[:, 32:] = up_ref[...]


def pick_kernel(slots_ref, mine_ref, other_ref, out_ref):
    x, c = lax.axis_index("x"), lax.axis_index("c")
    for to in range(Z):
        slot = slots_ref[to]
        owner = lax.rem(lax.div(slot, 2), X * C)
        dx = lax.rem(lax.div(owner, C) - x + X, X)
        block = jnp.where(dx == 0, 0, jnp.where(dx == 3, 1, jnp.where(dx == 1, 2, 3)))
        at = block * 2 + lax.rem(slot, 2)

        @pl.when(lax.rem(owner, C) == c)
        def _(to=to, at=at):
            out_ref[to] = mine_ref[at]

        @pl.when(lax.rem(owner, C) != c)
        def _(to=to, at=at):
            out_ref[to] = other_ref[at]


def bf16(*shape):
    return jax.ShapeDtypeStruct(shape, jnp.bfloat16)


def small(kernel, name, out_shape, scalars, *arrays):
    smem, vmem = pl.BlockSpec(memory_space=pltpu.SMEM), pl.BlockSpec(memory_space=pltpu.VMEM)
    return pl.pallas_call(
        kernel,
        out_shape=out_shape,
        in_specs=[smem] * len(scalars) + [vmem] * len(arrays),
        out_specs=[vmem] * len(out_shape),
        cost_estimate=pl.CostEstimate(flops=0, bytes_accessed=2 << 20, transcendentals=0),
        name=name,
    )(*scalars, *arrays)


def base_kernel(rows_ref, mine_ref, mine_close_ref, mine_far_ref, other_ref, other_close_ref, other_far_ref, out_ref, rows, weight, row_sems, weight_sems):
    x, c = lax.axis_index("x"), lax.axis_index("c")
    copies = []
    for j in range(Z):
        here = [pltpu.make_async_copy(rows_ref.at[:, pl.ds(j * 512, 512)], rows.at[j], row_sems.at[j])]
        sides = ((mine_ref, mine_close_ref, mine_far_ref), (other_ref, other_close_ref, other_far_ref))
        for s, (here_ref, close_ref, far_ref) in enumerate(sides):
            for q, dx in enumerate(QUAD):
                to = (lax.rem(x + dx + X, X) * C + lax.rem(c + s, C)) * 64
                here.append(
                    pltpu.make_async_copy(
                        (here_ref, close_ref, close_ref, far_ref)[q].at[pl.ds(((q == 2) * Z + j) * 64, 64)],
                        weight.at[j, pl.ds(pl.multiple_of(to, 64), 64)],
                        weight_sems.at[j * 8 + s * 4 + q],
                    )
                )
        for copy in here:
            copy.start()
        copies.append(here)
    for j in range(Z):
        for copy in copies[j]:
            copy.wait()
        term = jnp.dot(rows[j], weight[j], preferred_element_type=jnp.float32)
        if j == 0:
            out_ref[...] = term
        else:
            out_ref[...] += term


def adapt_kernel(length_ref, rows_ref, base_ref, adapters, out_ref, rows, row_sems):
    copies = [
        pltpu.make_async_copy(rows_ref.at[:, pl.ds(y * 512, 512)], rows.at[y], row_sems.at[y]) for y in range(Y)
    ]
    for copy in copies:
        copy.start()
    low = jnp.zeros((32, 512), jnp.float32)
    for y in range(Y):
        copies[y].wait()
        low += lax.dot_general(adapters[y, :32], rows[y], (((1,), (1,)), ((), ())), preferred_element_type=jnp.float32)
    low = low.astype(jnp.bfloat16)
    total = base_ref[...] + lax.dot_general(
        low, adapters[lax.axis_index("y"), 32:], (((0,), (0,)), ((), ())), preferred_element_type=jnp.float32
    )
    valid = lax.broadcasted_iota(jnp.int32, total.shape, 0) < length_ref[0]
    out_ref[...] = jnp.where(valid, total, 0.0).astype(jnp.bfloat16)


def per_device(
    prompts,
    layer_norm_gain,
    query_base_matrix,
    adapter_down_weight,
    adapter_up_weight,
    request_prompt_length,
    request_adapter_ident,
    adapter_pool_row,
):
    rows, noted, own = small(
        prepare_kernel,
        "prepare",
        (bf16(64, 4096), bf16(Z, 80, 512), bf16(2, 64, 512)),
        (request_adapter_ident, adapter_pool_row),
        prompts,
        layer_norm_gain.reshape(1, -1),
        query_base_matrix,
        adapter_down_weight,
        adapter_up_weight,
    )
    normed = lax.all_gather(rows, "y", axis=0, tiled=True)
    ring = lax.all_to_all(noted, "z", 0, 0)
    plane = jnp.concatenate([own, shift(own, dx=1), shift(own, dx=-1), shift(own, dx=2)], axis=0)
    plane_other = swap(plane)
    slots, weight = ring[:, 64, 0].astype(jnp.int32), ring[:, :64].reshape(512, 512)
    (wanted,) = small(pick_kernel, "pick", (bf16(Z, 64, 512),), (slots,), plane, plane_other)

    planes = lax.all_to_all(wanted, "z", 0, 0)
    weight_other = swap(after(weight, wanted))
    weight = after(weight, weight_other)
    from_left, from_right = shift(weight, dx=1), shift(weight, dx=-1)
    core = lax.axis_index("c")
    far_pairs = [p for p in req_pairs(dx=1) if p[0] % C == 0] + [p for p in req_pairs(dx=-1) if p[0] % C == 1]
    adapter = lax.dynamic_index_in_dim(planes, slots[lax.axis_index("z")] // (2 * X * C), 0, keepdims=False)
    spread = jnp.broadcast_to(adapter, (Y, 64, 512))
    adapters = lax.all_to_all(spread, "y", 0, 0)
    far = lax.ppermute(after(jnp.where(core == 0, from_left, from_right), spread), REQ, far_pairs)
    close = jnp.concatenate([from_left, from_right], axis=0)
    sides = ((weight, close, far), (weight_other, swap(close), swap(far)))

    any_space, vmem = pl.BlockSpec(memory_space=pl.ANY), pl.BlockSpec(memory_space=pltpu.VMEM)
    total = pl.pallas_call(
        base_kernel,
        out_shape=jax.ShapeDtypeStruct((512, 512), jnp.float32),
        in_specs=[any_space] * 7,
        out_specs=vmem,
        scratch_shapes=[
            pltpu.VMEM((8, 512, 512), jnp.bfloat16),
            pltpu.VMEM((8, 512, 512), jnp.bfloat16),
            pltpu.SemaphoreType.DMA((8,)),
            pltpu.SemaphoreType.DMA((64,)),
        ],
        compiler_params=pltpu.CompilerParams(vmem_limit_bytes=60 * 1024 * 1024),
        cost_estimate=pl.CostEstimate(flops=2 * 512 * 4096 * 512, bytes_accessed=9 << 20, transcendentals=0),
        name="base",
    )(normed, *sides[0], *sides[1])
    return pl.pallas_call(
        adapt_kernel,
        out_shape=bf16(512, 512),
        in_specs=[pl.BlockSpec(memory_space=pltpu.SMEM), any_space] + [vmem] * 2,
        out_specs=vmem,
        scratch_shapes=[pltpu.VMEM((8, 512, 512), jnp.bfloat16), pltpu.SemaphoreType.DMA((8,))],
        compiler_params=pltpu.CompilerParams(vmem_limit_bytes=60 * 1024 * 1024),
        cost_estimate=pl.CostEstimate(flops=2 * 512 * 4096 * 32, bytes_accessed=6 << 20, transcendentals=0),
        name="adapt",
    )(request_prompt_length, normed, total, adapters)


def solution(mesh):
    mesh = jax.sharding.Mesh(mesh.devices.reshape(Z, X, C, Y), (*REQ, "y"))
    in_specs = (
        P((*REQ, "y"), None),
        P(),
        P(REQ, "y"),
        P(REQ, None, "y"),
        P(REQ, None, "y"),
        P(REQ),
        P(REQ),
        P(),
    )
    return jax.shard_map(
        per_device, mesh=mesh, in_specs=in_specs, out_specs=P(REQ, "y"), check_vma=False
    )
```
